32 devices in a mesh: ctx: 16 (over z, y, x), dp: 2 (over core).
Axes of the slice: x: 2, y: 2, z: 4, core: 2. Of those that a mesh axis runs over, the one named last changes fastest.
Arguments:
- query_rows: bfloat16 [8192, 1024], P(('dp', 'ctx')), parts along dimension 0, may hold values from -100 to 100
- key_rows: bfloat16 [8192, 1024], P(('dp', 'ctx')), parts along dimension 0, may hold values from -5 to 5
- value_rows: bfloat16 [8192, 1024], P(('dp', 'ctx')), parts along dimension 0, may hold values from -6 to 6
- channels: bfloat16 [8192, 2048], P(('dp', 'ctx')), parts along dimension 0, may hold values from -6 to 6
- step_low: bfloat16 [8192, 128], P(('dp', 'ctx')), parts along dimension 0, may hold values from -6 to 6
- step_proj: bfloat16 [128, 2048], replicated, may hold values from -0.5 to 0.5
- step_bias: float32 [2048], replicated, may hold values from -8 to -2.5
- decay_log: float32 [16, 2048], replicated, may hold values from -6.5 to -0.5
- state_maps: float32 [2, 16, 8192], P(None, None, ('dp', 'ctx')), parts along dimension 2, may hold values from -6 to 6
- attend_weight: bfloat16 [1024, 128], replicated, may hold values from -0.5 to 0.5
- mixer_weight: bfloat16 [2048, 128], replicated, may hold values from -0.125 to 0.125
Outputs:
- token_vectors: bfloat16 [8192, 128], P(('dp', 'ctx')), parts along dimension 0
The draws below stay inside these ranges and needn't reach their ends.
There are 2 independent parts, one for each index of `dp`. The reference program is written for one: setup_inputs(seed, part) draws one part's arguments, and reference() takes and returns one part's arrays. A program takes and returns all parts, laid end to end along the dimension named above; an argument that names none is the same for every part. Nothing has to cross between parts.
All inputs are finite; a program needn't handle non-finite values.
Results may differ from the reference program's by a relative error of at most 0.005.
Values may be sent and summed in bfloat16 or wider, within the bound.
A program may use at most 128 MiB of HBM per device.

```python
import math
import jax
import jax.numpy as jnp
from jax import lax

HEADS = 8
HD = 128
CH = 2048
NS = 16
RANK = 128
EMB = 128
TOK_DEV = 256
SEQ = 4096
N_CTX = 16


def attention_pair(key):
    splits = jax.random.split(key, 2)
    feature_count = HEADS * HD
    query_base = jnp.clip(jax.random.normal(splits[0], (SEQ, feature_count), jnp.float32) * 1.2, -4.8, 4.8)
    key_base = jnp.clip(jax.random.normal(splits[1], (SEQ, feature_count), jnp.float32) * 1.2, -4.8, 4.8)
    return (query_base, key_base)


def draw_query_rows(key, part):
    return attention_pair(jax.random.fold_in(key, 11))[0].astype(jnp.bfloat16)


def draw_key_rows(key, part):
    return attention_pair(jax.random.fold_in(key, 11))[1].astype(jnp.bfloat16)


def mixer_rates(key):
    splits = jax.random.split(key, 4)
    share = 0.5
    slow_mask = jax.random.uniform(splits[0], (CH,), jnp.float32) < share
    slow_target = jnp.exp(jax.random.uniform(splits[1], (CH,), jnp.float32, math.log(0.2), math.log(2.0))) / SEQ
    fast_target = jnp.exp(jax.random.uniform(splits[2], (CH,), jnp.float32, math.log(0.1 / TOK_DEV), math.log(1.0 / 35.0)))
    target = jnp.where(slow_mask, slow_target, fast_target)
    spread = jnp.exp(jax.random.uniform(splits[3], (NS, CH), jnp.float32, math.log(0.6), math.log(1.6)))
    bias = jnp.log(0.5 * jnp.sqrt(target)) - 0.5
    rates = 2.0 * jnp.sqrt(target)[None, :] * spread
    return (bias, jnp.log(rates))


def draw_step_bias(key, part):
    return mixer_rates(jax.random.fold_in(key, 23))[0]


def draw_decay_log(key, part):
    return mixer_rates(jax.random.fold_in(key, 23))[1]


def shard_levels(rng, shape, cuts, low, high):
    def one(position, blocks):
        draws = jax.random.uniform(jax.random.fold_in(jax.random.fold_in(rng, 6), position), (blocks,), jnp.float32, low / len(cuts), high / len(cuts))
        return jnp.repeat(jnp.exp(draws), shape[position] // blocks).reshape((-1,) + (1,) * (len(shape) - position - 1))

    factor_of = one(*cuts[0])
    for cut in cuts[1:]:
        factor_of = factor_of * one(*cut)
    return factor_of


def gaussian(rng, extent, deviation, limit, cuts=(), held_as=jnp.bfloat16):
    values = deviation * jax.random.normal(rng, extent, jnp.float32)
    if cuts:
        values = values * shard_levels(rng, extent, cuts, -0.22, 0.18)
    return jnp.clip(values, -limit, limit).astype(held_as)


def setup_inputs(seed: int = 0, part: int = 0) -> dict:
    seeds = jax.random.split(jax.random.key(seed), 12)
    own_keys = jax.random.split(jax.random.fold_in(seeds[11], part), 12)
    return {
        "query_rows": draw_query_rows(jax.random.fold_in(jax.random.fold_in(seeds[11], part), 71), part),
        "key_rows": draw_key_rows(jax.random.fold_in(jax.random.fold_in(seeds[11], part), 71), part),
        "value_rows": gaussian(own_keys[2], (SEQ, HEADS * HD), 1.0, 6.0, ((0, 16),)),
        "channels": gaussian(own_keys[3], (SEQ, CH), 1.0, 6.0, ((0, 16),)),
        "step_low": gaussian(own_keys[4], (SEQ, RANK), 1.0, 6.0, ((0, 16),)),
        "step_proj": gaussian(seeds[5], (RANK, CH), RANK ** -0.5, 0.5),
        "step_bias": draw_step_bias(jax.random.fold_in(seeds[11], 71), part),
        "decay_log": draw_decay_log(jax.random.fold_in(seeds[11], 71), part),
        "state_maps": gaussian(own_keys[8], (2, NS, SEQ), 1.0, 6.0, ((2, 16),), jnp.float32),
        "attend_weight": gaussian(seeds[9], (HEADS * HD, EMB), HD ** -0.5, 0.5),
        "mixer_weight": gaussian(seeds[10], (CH, EMB), CH ** -0.5, 0.125),
    }


def attend_all(query_rows, key_rows, value_rows):
    feature_count = query_rows.shape[1]
    head_count = feature_count // HD
    window_rows = 4 * TOK_DEV
    pad_keys = jnp.concatenate([jnp.zeros((window_rows, feature_count), key_rows.dtype), key_rows], 0)
    pad_values = jnp.concatenate([jnp.zeros((window_rows, feature_count), value_rows.dtype), value_rows], 0)
    query_pos = jnp.arange(TOK_DEV, dtype=jnp.int32)[:, None]
    column = jnp.arange(5 * TOK_DEV, dtype=jnp.int32)[None, :]
    offset = column - window_rows
    base_mask = (offset <= query_pos) & (query_pos - offset < window_rows)

    def one_block(block_index):
        first_row = (block_index * TOK_DEV).astype(jnp.int32)
        query_block = lax.dynamic_slice_in_dim(query_rows, first_row, TOK_DEV, 0).astype(jnp.float32).reshape(TOK_DEV, head_count, HD)
        key_block = lax.dynamic_slice_in_dim(pad_keys, first_row, 5 * TOK_DEV, 0).astype(jnp.float32).reshape(5 * TOK_DEV, head_count, HD)
        value_block = lax.dynamic_slice_in_dim(pad_values, first_row, 5 * TOK_DEV, 0).astype(jnp.float32).reshape(5 * TOK_DEV, head_count, HD)
        scores = jnp.einsum('qhd,khd->hqk', query_block, key_block) * (1.0 / math.sqrt(HD))
        allowed = base_mask & (first_row + offset >= 0)
        scores = jnp.where(allowed[None], scores, -1e+30)
        row_max = lax.optimization_barrier(jnp.max(scores, -1, keepdims=True))
        exp_terms = jnp.exp(scores - row_max)
        row_sum = lax.optimization_barrier(jnp.sum(exp_terms, -1))
        rounded = lax.optimization_barrier(exp_terms.astype(jnp.bfloat16))
        weights = rounded.astype(jnp.float32)
        summed = jnp.einsum('hqk,khd->qhd', weights, value_block)
        result = summed / jnp.transpose(row_sum)[:, :, None]
        return result.reshape(TOK_DEV, feature_count).astype(jnp.bfloat16)
    blocks = lax.map(one_block, jnp.arange(N_CTX, dtype=jnp.int32))
    return blocks.reshape(SEQ, feature_count)

def mixer_all(channels, step_low, step_proj, step_bias, decay_log, state_maps):
    timestep = jax.nn.softplus(jnp.dot(step_low, step_proj, preferred_element_type=jnp.float32) + step_bias)
    decay_rate = -jnp.exp(decay_log)
    inflow = timestep * channels.astype(jnp.float32)

    def advance(carry_state, inputs):
        step_row, inflow_row, in_row, out_row = inputs
        carry_state = jnp.exp(step_row[None, :] * decay_rate) * carry_state + in_row[:, None] * inflow_row[None, :]
        return (carry_state, lax.optimization_barrier(jnp.sum(out_row[:, None] * carry_state, 0)))
    zero_state = jnp.zeros(decay_log.shape, jnp.float32)
    final_state, outputs = lax.scan(advance, zero_state, (timestep, inflow, jnp.transpose(state_maps[0]), jnp.transpose(state_maps[1])))
    return outputs

def reference(query_rows, key_rows, value_rows, channels, step_low, step_proj, step_bias, decay_log, state_maps, attend_weight, mixer_weight):
    mixer_out = mixer_all(channels, step_low, step_proj, step_bias, decay_log, state_maps)
    mixer_norm = (mixer_out * lax.rsqrt(lax.optimization_barrier(jnp.mean(mixer_out * mixer_out, -1, keepdims=True)) + 1e-05)).astype(jnp.bfloat16)
    attended = attend_all(query_rows, key_rows, value_rows)
    combined = jnp.dot(attended, attend_weight, preferred_element_type=jnp.float32) + jnp.dot(mixer_norm, mixer_weight, preferred_element_type=jnp.float32)
    return (combined * lax.rsqrt(lax.optimization_barrier(jnp.mean(combined * combined, -1, keepdims=True)) + 1e-06)).astype(jnp.bfloat16)
```

```python
import functools
import math

import jax
import jax.numpy as jnp
from jax import lax
from jax.experimental import pallas as pl
from jax.experimental.pallas import tpu as pltpu
from jax.sharding import PartitionSpec as P

HD = 128
LANES = 128
GROUP = 4
LOG2E = math.log2(math.e)


def nt_dot(a, b):
    return lax.dot_general(a, b, (((1,), (1,)), ((), ())), preferred_element_type=jnp.float32)


def block_kernel(
    n,
    q_hbm,
    k_hbm,
    v_hbm,
    ch_ref,
    low_ref,
    proj_ref,
    bias_ref,
    dlog_ref,
    maps_ref,
    aw_ref,
    mw_ref,
    out_ref,
    qb,
    kb,
    vb,
    pk,
    pv,
    att,
    stage,
    dts,
    us,
    decays,
    rate,
    msg_out,
    msg_in,
    local_sem,
    plane_send,
    plane_recv,
    next_send,
    next_recv,
    state_send,
    state_recv,
    att_send,
    att_recv,
):
    rows, feats = q_hbm.shape
    width = feats // GROUP
    heads_here = width // HD
    ns = dlog_ref.shape[0]
    cb = dlog_ref.shape[1] // LANES
    state_rows = ns * cb
    me = lax.axis_index("ctx")
    group = lax.div(me, GROUP)
    place = lax.rem(me, GROUP)
    base = group * GROUP
    hops = []
    while 2 ** len(hops) < n:
        hops.append(2 ** len(hops))

    barrier = pltpu.get_barrier_semaphore()
    greeted = 0
    for r in range(1, GROUP):
        pl.semaphore_signal(barrier, inc=1, device_id={"ctx": base + lax.rem(place + r, GROUP)})
        greeted += 1
    for d in hops:
        pl.semaphore_signal(barrier, inc=1, device_id={"ctx": lax.rem(me + d, n)})
        pl.semaphore_signal(barrier, inc=1, device_id={"ctx": lax.rem(me + n - d, n)})
        greeted += 2
    pl.semaphore_wait(barrier, greeted)

    def columns(where):
        return pl.ds(pl.multiple_of(where * width, LANES), width)

    def block(where):
        return pl.ds(pl.multiple_of(where * rows, rows), rows)

    pairs = ((k_hbm, kb, pk), (v_hbm, vb, pv), (q_hbm, qb, None))

    def plane_copy(a, r):
        there = lax.rem(place + r, GROUP)
        source, buffer, _ = pairs[a]
        return pltpu.make_async_remote_copy(
            src_ref=source.at[:, columns(there)],
            dst_ref=buffer.at[block(place), :],
            send_sem=plane_send.at[a, r],
            recv_sem=plane_recv.at[a, r],
            device_id={"ctx": base + there},
        )

    def own_copy(a):
        source, buffer, _ = pairs[a]
        return pltpu.make_async_copy(
            source.at[:, columns(place)], buffer.at[block(place), :], local_sem.at[a]
        )

    def next_copy(a, r):
        source, buffer, far = pairs[a]
        which = lax.rem(place + GROUP - r, GROUP)
        return pltpu.make_async_remote_copy(
            src_ref=source.at[:, columns(place)] if r == 0 else buffer.at[block(which), :],
            dst_ref=far.at[block(which), :],
            send_sem=next_send.at[a, r],
            recv_sem=next_recv.at[a, r],
            device_id={"ctx": lax.rem(me + GROUP, n)},
        )

    has_next = me + GROUP < n
    has_before = group > 0

    for a in range(2):
        for r in range(1, GROUP):
            plane_copy(a, r).start()
    if n > GROUP:

        @pl.when(has_next)
        def _():
            for a in range(2):
                next_copy(a, 0).start()

    for a in range(3):
        own_copy(a).start()

    for j in range(cb):
        cols = slice(j * LANES, (j + 1) * LANES)
        rate[pl.ds(j, ns, stride=cb), :] = -jnp.exp(dlog_ref[:, cols]) * LOG2E
    for j in range(cb):
        cols = slice(j * LANES, (j + 1) * LANES)
        raw = jnp.dot(low_ref[...], proj_ref[:, cols], preferred_element_type=jnp.float32)
        raw = raw + bias_ref[:, cols]
        step = jnp.maximum(raw, 0.0) + jnp.log1p(jnp.exp(-jnp.abs(raw)))
        dts[pl.ds(j, rows, stride=cb), :] = step
        us[pl.ds(j, rows, stride=cb), :] = step * ch_ref[:, cols].astype(jnp.float32)

    def first_pass(t, carry):
        total, state = carry[0], carry[1:]
        here = pl.ds(pl.multiple_of(t * cb, cb), cb)
        step = dts[here, :]
        flow = us[here, :]
        new = []
        for s in range(ns):
            decay = jnp.exp2(step * rate[s * cb : (s + 1) * cb, :])
            decays[pl.ds(pl.multiple_of(t * state_rows, cb) + s * cb, cb), :] = decay
            new.append(decay * state[s] + maps_ref[0, s, t] * flow)
        return (total + step, *new)

    zero = jnp.zeros((cb, LANES), jnp.float32)
    carry = (zero,) * (ns + 1)

    def forward(r):
        for a in range(2):
            plane_copy(a, r).wait_recv()

        @pl.when(has_next)
        def _():
            for a in range(2):
                next_copy(a, r).start()

    cuts = [0, rows // 2, 3 * rows // 4, rows]
    for r in range(1, GROUP):
        carry = lax.fori_loop(cuts[r - 1], cuts[r], first_pass, carry)
        if n > GROUP:
            forward(r)
        else:
            for a in range(2):
                plane_copy(a, r).wait_recv()

    def state_copy(k, d):
        return pltpu.make_async_remote_copy(
            src_ref=msg_out.at[k],
            dst_ref=msg_in.at[k],
            send_sem=state_send.at[k],
            recv_sem=state_recv.at[k],
            device_id={"ctx": lax.rem(me + d, n)},
        )

    def spread(total):
        return jnp.concatenate([total] * ns, 0)

    held = jnp.concatenate(carry[1:], 0)
    total = carry[0]
    msg_out[0, :state_rows, :] = held
    msg_out[0, state_rows:, :] = total
    before = msg_out.at[len(hops)]
    before[...] = jnp.zeros_like(before)
    for k, d in enumerate(hops):

        @pl.when(me + d < n)
        def _():
            state_copy(k, d).start()

        if k == 0:
            for r in range(1, GROUP):
                plane_copy(2, r).start()
        last = k + 1 == len(hops)
        if not last:
            msg_out[k + 1] = msg_out[k]

        @pl.when(me >= d)
        def _():
            state_copy(k, d).wait_recv()
            arrived = msg_in[k, :state_rows, :]
            arrived_total = msg_in[k, state_rows:, :]
            spans = before[state_rows:, :]
            before[:state_rows, :] = (
                jnp.exp2(rate[...] * spread(spans)) * arrived + before[:state_rows, :]
            )
            before[state_rows:, :] = spans + arrived_total
            if not last:
                spans = msg_out[k, state_rows:, :]
                msg_out[k + 1, :state_rows, :] = (
                    jnp.exp2(rate[...] * spread(spans)) * arrived + msg_out[k, :state_rows, :]
                )
                msg_out[k + 1, state_rows:, :] = spans + arrived_total

    def second_pass(t, state):
        here = pl.ds(pl.multiple_of(t * cb, cb), cb)
        flow = us[here, :]
        new = []
        out = None
        for s in range(ns):
            decay = decays[pl.ds(pl.multiple_of(t * state_rows, cb) + s * cb, cb), :]
            value = decay * state[s] + maps_ref[0, s, t] * flow
            new.append(value)
            term = maps_ref[1, s, t] * value
            out = term if out is None else out + term
        dts[here, :] = out
        return tuple(new)

    lax.fori_loop(
        0,
        rows,
        second_pass,
        tuple(before[s * cb : (s + 1) * cb, :] for s in range(ns)),
    )

    squares = jnp.zeros((rows, LANES), jnp.float32)
    for j in range(cb):
        part = dts[pl.ds(j, rows, stride=cb), :]
        squares = squares + part * part
    scale = lax.rsqrt(jnp.sum(squares, -1, keepdims=True) / (cb * LANES) + 1e-05)
    combined = jnp.zeros((rows, out_ref.shape[1]), jnp.float32)
    for j in range(cb):
        part = (dts[pl.ds(j, rows, stride=cb), :] * scale).astype(jnp.bfloat16)
        combined = combined + jnp.dot(
            part, mw_ref[j * LANES : (j + 1) * LANES, :], preferred_element_type=jnp.float32
        )

    for a in range(3):
        own_copy(a).wait()
    for r in range(1, GROUP):
        plane_copy(2, r).wait_recv()
    if n > GROUP:

        @pl.when(has_before)
        def _():
            for r in range(GROUP):
                for a in range(2):
                    next_copy(a, r).wait_recv()

    @pl.when(group == 0)
    def _():
        pk[...] = jnp.zeros_like(pk)
        pv[...] = jnp.zeros_like(pv)

    def att_copy(s):
        return pltpu.make_async_remote_copy(
            src_ref=stage.at[s],
            dst_ref=att.at[place],
            send_sem=att_send.at[s],
            recv_sem=att_recv.at[place],
            device_id={"ctx": base + s},
        )

    shut = jnp.where(has_before, 0, GROUP * rows).astype(jnp.int32)
    for s in range(GROUP):
        near = (s + 1) * rows
        far = (GROUP - s) * rows
        near_open = lax.broadcasted_iota(jnp.int32, (rows, near), 1) <= (
            lax.broadcasted_iota(jnp.int32, (rows, near), 0) + s * rows
        )
        far_open = lax.broadcasted_iota(jnp.int32, (rows, far), 1) > (
            lax.broadcasted_iota(jnp.int32, (rows, far), 0) + shut
        )
        for h in range(heads_here):
            cols = slice(h * HD, (h + 1) * HD)
            query = qb[s * rows : (s + 1) * rows, cols]
            factor = LOG2E / math.sqrt(HD)
            near_scores = nt_dot(query, kb[:near, cols]) * factor
            far_scores = nt_dot(query, pk[s * rows :, cols]) * factor
            near_scores = jnp.where(near_open, near_scores, -1e30)
            far_scores = jnp.where(far_open, far_scores, -1e30)
            top = jnp.maximum(
                jnp.max(near_scores, -1, keepdims=True), jnp.max(far_scores, -1, keepdims=True)
            )
            near_terms = jnp.exp2(near_scores - top)
            far_terms = jnp.exp2(far_scores - top)
            row_sum = jnp.sum(near_terms, -1, keepdims=True) + jnp.sum(
                far_terms, -1, keepdims=True
            )
            summed = jnp.dot(
                near_terms.astype(jnp.bfloat16), vb[:near, cols], preferred_element_type=jnp.float32
            ) + jnp.dot(
                far_terms.astype(jnp.bfloat16),
                pv[s * rows :, cols],
                preferred_element_type=jnp.float32,
            )
            stage[s, :, cols] = (summed / row_sum).astype(jnp.bfloat16)

        @pl.when(place != s)
        def _():
            att_copy(s).start()

    for s in range(GROUP):

        @pl.when(place != s)
        def _():
            pltpu.make_async_remote_copy(
                src_ref=stage.at[s],
                dst_ref=att.at[s],
                send_sem=att_send.at[s],
                recv_sem=att_recv.at[s],
                device_id={"ctx": base + s},
            ).wait_recv()

        @pl.when(place == s)
        def _():
            att[s] = stage[s]

    for s in range(GROUP):
        combined = combined + jnp.dot(
            att[s], aw_ref[s * width : (s + 1) * width, :], preferred_element_type=jnp.float32
        )
    mean = jnp.mean(combined * combined, -1, keepdims=True)
    out_ref[...] = (combined * lax.rsqrt(mean + 1e-06)).astype(out_ref.dtype)

    for a in range(3):
        for r in range(1, GROUP):
            plane_copy(a, r).wait_send()
    if n > GROUP:

        @pl.when(has_next)
        def _():
            for r in range(GROUP):
                for a in range(2):
                    next_copy(a, r).wait_send()

    for k, d in enumerate(hops):

        @pl.when(me + d < n)
        def _():
            state_copy(k, d).wait_send()

    for s in range(GROUP):

        @pl.when(place != s)
        def _():
            att_copy(s).wait_send()


def per_device(
    n,
    query_rows,
    key_rows,
    value_rows,
    channels,
    step_low,
    step_proj,
    step_bias,
    decay_log,
    state_maps,
    attend_weight,
    mixer_weight,
):
    rows, feats = query_rows.shape
    width = feats // GROUP
    ns, ch = decay_log.shape
    cb = ch // LANES
    rounds = max(1, (n - 1).bit_length())
    any_spec = pl.BlockSpec(memory_space=pl.ANY)
    vmem = pl.BlockSpec(memory_space=pltpu.VMEM)
    smem = pl.BlockSpec(memory_space=pltpu.SMEM)
    wide = pltpu.VMEM((GROUP * rows, width), jnp.bfloat16)
    dma = pltpu.SemaphoreType.DMA
    return pl.pallas_call(
        functools.partial(block_kernel, n),
        out_shape=jax.ShapeDtypeStruct((rows, attend_weight.shape[1]), jnp.bfloat16),
        in_specs=[any_spec] * 3 + [vmem] * 5 + [smem] + [vmem] * 2,
        out_specs=vmem,
        scratch_shapes=[
            wide,
            wide,
            wide,
            wide,
            wide,
            pltpu.VMEM((GROUP, rows, width), jnp.bfloat16),
            pltpu.VMEM((GROUP, rows, width), jnp.bfloat16),
            pltpu.VMEM((rows * cb, LANES), jnp.float32),
            pltpu.VMEM((rows * cb, LANES), jnp.float32),
            pltpu.VMEM((rows * ns * cb, LANES), jnp.float32),
            pltpu.VMEM((ns * cb, LANES), jnp.float32),
            pltpu.VMEM((rounds + 1, (ns + 1) * cb, LANES), jnp.float32),
            pltpu.VMEM((rounds, (ns + 1) * cb, LANES), jnp.float32),
            dma((3,)),
            dma((3, GROUP)),
            dma((3, GROUP)),
            dma((2, GROUP)),
            dma((2, GROUP)),
            dma((rounds,)),
            dma((rounds,)),
            dma((GROUP,)),
            dma((GROUP,)),
        ],
        compiler_params=pltpu.CompilerParams(
            collective_id=0, has_side_effects=True, vmem_limit_bytes=60 * 1024 * 1024
        ),
    )(
        query_rows,
        key_rows,
        value_rows,
        channels,
        step_low,
        step_proj,
        step_bias.reshape(1, -1),
        decay_log,
        state_maps,
        attend_weight,
        mixer_weight,
    )


def solution(mesh):
    return jax.shard_map(
        functools.partial(per_device, mesh.shape["ctx"]),
        mesh=mesh,
        in_specs=(
            P(("dp", "ctx"), None),
            P(("dp", "ctx"), None),
            P(("dp", "ctx"), None),
            P(("dp", "ctx"), None),
            P(("dp", "ctx"), None),
            P(),
            P(),
            P(),
            P(None, None, ("dp", "ctx")),
            P(),
            P(),
        ),
        out_specs=P(("dp", "ctx"), None),
        check_vma=False,
    )
```

```python
import functools
import math

import jax
import jax.numpy as jnp
from jax import lax
from jax.experimental import pallas as pl
from jax.experimental.pallas import tpu as pltpu
from jax.sharding import PartitionSpec as P

HD = 128
LANES = 128
GROUP = 4
LOG2E = math.log2(math.e)


def nt_dot(a, b):
    return lax.dot_general(a, b, (((1,), (1,)), ((), ())), preferred_element_type=jnp.float32)


def block_kernel(
    n,
    q_hbm,
    k_hbm,
    v_hbm,
    ch_ref,
    low_ref,
    proj_ref,
    bias_ref,
    dlog_ref,
    maps_ref,
    aw_ref,
    mw_ref,
    out_ref,
    qb,
    kb,
    vb,
    pk,
    pv,
    att,
    stage,
    dts,
    us,
    decays,
    rate,
    quarter_out,
    quarter_in,
    far_out,
    far_in,
    enter_out,
    enter,
    local_sem,
    plane_send,
    plane_recv,
    next_send,
    next_recv,
    quarter_send,
    quarter_recv,
    far_send,
    far_recv,
    enter_send,
    enter_recv,
    att_send,
    att_recv,
):
    rows, feats = q_hbm.shape
    width = feats // GROUP
    heads_here = width // HD
    ns = dlog_ref.shape[0]
    cb = dlog_ref.shape[1] // LANES
    state_rows = ns * cb
    me = lax.axis_index("ctx")
    group = lax.div(me, GROUP)
    place = lax.rem(me, GROUP)
    base = group * GROUP
    hops = []
    while GROUP * 2 ** len(hops) < n:
        hops.append(GROUP * 2 ** len(hops))

    barrier = pltpu.get_barrier_semaphore()
    greeted = 0
    for r in range(1, GROUP):
        pl.semaphore_signal(barrier, inc=1, device_id={"ctx": base + lax.rem(place + r, GROUP)})
        greeted += 1
    for d in hops:
        pl.semaphore_signal(barrier, inc=1, device_id={"ctx": lax.rem(me + d, n)})
        pl.semaphore_signal(barrier, inc=1, device_id={"ctx": lax.rem(me + n - d, n)})
        greeted += 2
    pl.semaphore_wait(barrier, greeted)

    def columns(where):
        return pl.ds(pl.multiple_of(where * width, LANES), width)

    def block(where):
        return pl.ds(pl.multiple_of(where * rows, rows), rows)

    pairs = ((k_hbm, kb, pk), (v_hbm, vb, pv), (q_hbm, qb, None))

    def plane_copy(a, r):
        there = lax.rem(place + r, GROUP)
        source, buffer, _ = pairs[a]
        return pltpu.make_async_remote_copy(
            src_ref=source.at[:, columns(there)],
            dst_ref=buffer.at[block(place), :],
            send_sem=plane_send.at[a, r],
            recv_sem=plane_recv.at[a, r],
            device_id={"ctx": base + there},
        )

    def own_copy(a):
        source, buffer, _ = pairs[a]
        return pltpu.make_async_copy(
            source.at[:, columns(place)], buffer.at[block(place), :], local_sem.at[a]
        )

    def next_copy(a, r):
        source, buffer, far = pairs[a]
        which = lax.rem(place + GROUP - r, GROUP)
        return pltpu.make_async_remote_copy(
            src_ref=source.at[:, columns(place)] if r == 0 else buffer.at[block(which), :],
            dst_ref=far.at[block(which), :],
            send_sem=next_send.at[a, r],
            recv_sem=next_recv.at[a, r],
            device_id={"ctx": lax.rem(me + GROUP, n)},
        )

    has_next = me + GROUP < n
    has_before = group > 0

    for a in range(2):
        for r in range(1, GROUP):
            plane_copy(a, r).start()
    if n > GROUP:

        @pl.when(has_next)
        def _():
            for a in range(2):
                next_copy(a, 0).start()

    for a in range(3):
        own_copy(a).start()
    for r in range(1, GROUP):
        plane_copy(2, r).start()

    for j in range(cb):
        cols = slice(j * LANES, (j + 1) * LANES)
        rate[pl.ds(j, ns, stride=cb), :] = -jnp.exp(dlog_ref[:, cols]) * LOG2E
    for j in range(cb):
        cols = slice(j * LANES, (j + 1) * LANES)
        raw = jnp.dot(low_ref[...], proj_ref[:, cols], preferred_element_type=jnp.float32)
        raw = raw + bias_ref[:, cols]
        step = jnp.maximum(raw, 0.0) + jnp.log1p(jnp.exp(-jnp.abs(raw)))
        dts[pl.ds(j, rows, stride=cb), :] = step
        us[pl.ds(j, rows, stride=cb), :] = step * ch_ref[:, cols].astype(jnp.float32)

    def first_pass(t, carry):
        total, state = carry[0], carry[1:]
        here = pl.ds(pl.multiple_of(t * cb, cb), cb)
        step = dts[here, :]
        flow = us[here, :]
        new = []
        for s in range(ns):
            decay = jnp.exp2(step * rate[s * cb : (s + 1) * cb, :])
            decays[pl.ds(pl.multiple_of(t * state_rows, cb) + s * cb, cb), :] = decay
            new.append(decay * state[s] + maps_ref[0, s, t] * flow)
        return (total + step, *new)

    zero = jnp.zeros((cb, LANES), jnp.float32)
    carry = (zero,) * (ns + 1)

    def forward(r):
        for a in range(2):
            plane_copy(a, r).wait_recv()

        @pl.when(has_next)
        def _():
            for a in range(2):
                next_copy(a, r).start()

    cuts = [0, rows // 2, 3 * rows // 4, rows]
    for r in range(1, GROUP):
        carry = lax.fori_loop(cuts[r - 1], cuts[r], first_pass, carry, unroll=2)
        if n > GROUP:
            forward(r)
        else:
            for a in range(2):
                plane_copy(a, r).wait_recv()

    part = state_rows // GROUP
    mine = pl.ds(pl.multiple_of(place * part, part), part)

    def quarter_copy(r):
        there = lax.rem(place + r, GROUP)
        return pltpu.make_async_remote_copy(
            src_ref=quarter_out.at[there],
            dst_ref=quarter_in.at[place],
            send_sem=quarter_send.at[r],
            recv_sem=quarter_recv.at[r],
            device_id={"ctx": base + there},
        )

    def far_copy(k, d):
        return pltpu.make_async_remote_copy(
            src_ref=far_out.at[k],
            dst_ref=far_in.at[k],
            send_sem=far_send.at[k],
            recv_sem=far_recv.at[k],
            device_id={"ctx": lax.rem(me + d, n)},
        )

    def enter_copy(r):
        there = lax.rem(place + r, GROUP)
        return pltpu.make_async_remote_copy(
            src_ref=enter_out.at[there],
            dst_ref=enter.at[mine, :],
            send_sem=enter_send.at[r],
            recv_sem=enter_recv.at[r],
            device_id={"ctx": base + there},
        )

    def through(spans):
        return jnp.exp2(rate[mine, :] * jnp.concatenate([spans] * (part // cb), 0))

    states_each = part // cb
    for q in range(GROUP):
        for i in range(states_each):
            quarter_out[q, i * cb : (i + 1) * cb, :] = carry[1 + q * states_each + i]
        quarter_out[q, part:, :] = carry[0]
    for r in range(1, GROUP):
        quarter_copy(r).start()
    quarter_in[place] = quarter_out[place]
    for r in range(1, GROUP):
        quarter_copy(r).wait_recv()

    run_state = jnp.zeros((part, LANES), jnp.float32)
    run_total = jnp.zeros((cb, LANES), jnp.float32)
    entries = []
    for q in range(GROUP):
        entries.append((run_state, run_total))
        spans = quarter_in[q, part:, :]
        run_state = through(spans) * run_state + quarter_in[q, :part, :]
        run_total = run_total + spans

    before = far_out.at[len(hops)]
    before[...] = jnp.zeros_like(before)
    if hops:
        far_out[0, :part, :] = run_state
        far_out[0, part:, :] = run_total
    for k, d in enumerate(hops):

        @pl.when(me + d < n)
        def _():
            far_copy(k, d).start()

        last = k + 1 == len(hops)
        if not last:
            far_out[k + 1] = far_out[k]

        @pl.when(me >= d)
        def _():
            far_copy(k, d).wait_recv()
            arrived = far_in[k, :part, :]
            arrived_total = far_in[k, part:, :]
            spans = before[part:, :]
            before[:part, :] = through(spans) * arrived + before[:part, :]
            before[part:, :] = spans + arrived_total
            if not last:
                spans = far_out[k, part:, :]
                far_out[k + 1, :part, :] = through(spans) * arrived + far_out[k, :part, :]
                far_out[k + 1, part:, :] = spans + arrived_total

    group_state = before[:part, :]
    for q in range(GROUP):
        enter_out[q] = through(entries[q][1]) * group_state + entries[q][0]
    for r in range(1, GROUP):
        enter_copy(r).start()
    enter[mine, :] = enter_out[place]

    for a in range(3):
        own_copy(a).wait()
    for r in range(1, GROUP):
        plane_copy(2, r).wait_recv()
    if n > GROUP:

        @pl.when(has_before)
        def _():
            for r in range(GROUP):
                for a in range(2):
                    next_copy(a, r).wait_recv()

    @pl.when(group == 0)
    def _():
        pk[...] = jnp.zeros_like(pk)
        pv[...] = jnp.zeros_like(pv)

    def att_copy(s):
        return pltpu.make_async_remote_copy(
            src_ref=stage.at[s],
            dst_ref=att.at[place],
            send_sem=att_send.at[s],
            recv_sem=att_recv.at[place],
            device_id={"ctx": base + s},
        )

    shut = jnp.where(has_before, 0, GROUP * rows).astype(jnp.int32)
    for s in range(GROUP):
        near = (s + 1) * rows
        far = (GROUP - s) * rows
        near_open = lax.broadcasted_iota(jnp.int32, (rows, near), 1) <= (
            lax.broadcasted_iota(jnp.int32, (rows, near), 0) + s * rows
        )
        far_open = lax.broadcasted_iota(jnp.int32, (rows, far), 1) > (
            lax.broadcasted_iota(jnp.int32, (rows, far), 0) + shut
        )
        for h in range(heads_here):
            cols = slice(h * HD, (h + 1) * HD)
            query = qb[s * rows : (s + 1) * rows, cols]
            factor = LOG2E / math.sqrt(HD)
            near_scores = nt_dot(query, kb[:near, cols]) * factor
            far_scores = nt_dot(query, pk[s * rows :, cols]) * factor
            near_scores = jnp.where(near_open, near_scores, -1e30)
            far_scores = jnp.where(far_open, far_scores, -1e30)
            top = jnp.maximum(
                jnp.max(near_scores, -1, keepdims=True), jnp.max(far_scores, -1, keepdims=True)
            )
            near_terms = jnp.exp2(near_scores - top)
            far_terms = jnp.exp2(far_scores - top)
            row_sum = jnp.sum(near_terms, -1, keepdims=True) + jnp.sum(
                far_terms, -1, keepdims=True
            )
            summed = jnp.dot(
                near_terms.astype(jnp.bfloat16), vb[:near, cols], preferred_element_type=jnp.float32
            ) + jnp.dot(
                far_terms.astype(jnp.bfloat16),
                pv[s * rows :, cols],
                preferred_element_type=jnp.float32,
            )
            stage[s, :, cols] = (summed / row_sum).astype(jnp.bfloat16)

        @pl.when(place != s)
        def _():
            att_copy(s).start()

    def second_pass(t, state):
        here = pl.ds(pl.multiple_of(t * cb, cb), cb)
        flow = us[here, :]
        new = []
        out = None
        for s in range(ns):
            decay = decays[pl.ds(pl.multiple_of(t * state_rows, cb) + s * cb, cb), :]
            value = decay * state[s] + maps_ref[0, s, t] * flow
            new.append(value)
            term = maps_ref[1, s, t] * value
            out = term if out is None else out + term
        dts[here, :] = out
        return tuple(new)

    for r in range(1, GROUP):
        enter_copy(r).wait_recv()
    lax.fori_loop(
        0,
        rows,
        second_pass,
        tuple(enter[s * cb : (s + 1) * cb, :] for s in range(ns)),
        unroll=2,
    )

    squares = jnp.zeros((rows, LANES), jnp.float32)
    for j in range(cb):
        part = dts[pl.ds(j, rows, stride=cb), :]
        squares = squares + part * part
    scale = lax.rsqrt(jnp.sum(squares, -1, keepdims=True) / (cb * LANES) + 1e-05)
    combined = jnp.zeros((rows, out_ref.shape[1]), jnp.float32)
    for j in range(cb):
        part = (dts[pl.ds(j, rows, stride=cb), :] * scale).astype(jnp.bfloat16)
        combined = combined + jnp.dot(
            part, mw_ref[j * LANES : (j + 1) * LANES, :], preferred_element_type=jnp.float32
        )

    for s in range(GROUP):

        @pl.when(place != s)
        def _():
            pltpu.make_async_remote_copy(
                src_ref=stage.at[s],
                dst_ref=att.at[s],
                send_sem=att_send.at[s],
                recv_sem=att_recv.at[s],
                device_id={"ctx": base + s},
            ).wait_recv()

        @pl.when(place == s)
        def _():
            att[s] = stage[s]

    for s in range(GROUP):
        combined = combined + jnp.dot(
            att[s], aw_ref[s * width : (s + 1) * width, :], preferred_element_type=jnp.float32
        )
    mean = jnp.mean(combined * combined, -1, keepdims=True)
    out_ref[...] = (combined * lax.rsqrt(mean + 1e-06)).astype(out_ref.dtype)

    for a in range(3):
        for r in range(1, GROUP):
            plane_copy(a, r).wait_send()
    if n > GROUP:

        @pl.when(has_next)
        def _():
            for r in range(GROUP):
                for a in range(2):
                    next_copy(a, r).wait_send()

    for r in range(1, GROUP):
        quarter_copy(r).wait_send()
        enter_copy(r).wait_send()
    for k, d in enumerate(hops):

        @pl.when(me + d < n)
        def _():
            far_copy(k, d).wait_send()

    for s in range(GROUP):

        @pl.when(place != s)
        def _():
            att_copy(s).wait_send()


def per_device(
    n,
    query_rows,
    key_rows,
    value_rows,
    channels,
    step_low,
    step_proj,
    step_bias,
    decay_log,
    state_maps,
    attend_weight,
    mixer_weight,
):
    rows, feats = query_rows.shape
    width = feats // GROUP
    ns, ch = decay_log.shape
    cb = ch // LANES
    rounds = max(1, (n // GROUP - 1).bit_length())
    part = ns * cb // GROUP
    any_spec = pl.BlockSpec(memory_space=pl.ANY)
    vmem = pl.BlockSpec(memory_space=pltpu.VMEM)
    smem = pl.BlockSpec(memory_space=pltpu.SMEM)
    wide = pltpu.VMEM((GROUP * rows, width), jnp.bfloat16)
    dma = pltpu.SemaphoreType.DMA
    return pl.pallas_call(
        functools.partial(block_kernel, n),
        out_shape=jax.ShapeDtypeStruct((rows, attend_weight.shape[1]), jnp.bfloat16),
        in_specs=[any_spec] * 3 + [vmem] * 5 + [smem] + [vmem] * 2,
        out_specs=vmem,
        scratch_shapes=[
            wide,
            wide,
            wide,
            wide,
            wide,
            pltpu.VMEM((GROUP, rows, width), jnp.bfloat16),
            pltpu.VMEM((GROUP, rows, width), jnp.bfloat16),
            pltpu.VMEM((rows * cb, LANES), jnp.float32),
            pltpu.VMEM((rows * cb, LANES), jnp.float32),
            pltpu.VMEM((rows * ns * cb, LANES), jnp.float32),
            pltpu.VMEM((ns * cb, LANES), jnp.float32),
            pltpu.VMEM((GROUP, part + cb, LANES), jnp.float32),
            pltpu.VMEM((GROUP, part + cb, LANES), jnp.float32),
            pltpu.VMEM((rounds + 1, part + cb, LANES), jnp.float32),
            pltpu.VMEM((rounds, part + cb, LANES), jnp.float32),
            pltpu.VMEM((GROUP, part, LANES), jnp.float32),
            pltpu.VMEM((ns * cb, LANES), jnp.float32),
            dma((3,)),
            dma((3, GROUP)),
            dma((3, GROUP)),
            dma((2, GROUP)),
            dma((2, GROUP)),
            dma((GROUP,)),
            dma((GROUP,)),
            dma((rounds,)),
            dma((rounds,)),
            dma((GROUP,)),
            dma((GROUP,)),
            dma((GROUP,)),
            dma((GROUP,)),
        ],
        compiler_params=pltpu.CompilerParams(
            collective_id=0, has_side_effects=True, vmem_limit_bytes=60 * 1024 * 1024
        ),
    )(
        query_rows,
        key_rows,
        value_rows,
        channels,
        step_low,
        step_proj,
        step_bias.reshape(1, -1),
        decay_log,
        state_maps,
        attend_weight,
        mixer_weight,
    )


def solution(mesh):
    return jax.shard_map(
        functools.partial(per_device, mesh.shape["ctx"]),
        mesh=mesh,
        in_specs=(
            P(("dp", "ctx"), None),
            P(("dp", "ctx"), None),
            P(("dp", "ctx"), None),
            P(("dp", "ctx"), None),
            P(("dp", "ctx"), None),
            P(),
            P(),
            P(),
            P(None, None, ("dp", "ctx")),
            P(),
            P(),
        ),
        out_specs=P(("dp", "ctx"), None),
        check_vma=False,
    )
```
